256 devices in a mesh: section: 16 (over y, x_lo, core), tensor: 8 (over z), dp: 2 (over x_hi).
Axes of the slice: x: 4 (x_hi: 2, x_lo: 2; x = x_hi * 2 + x_lo), y: 4, z: 8, core: 2. Of those that a mesh axis runs over, the one named last changes fastest.
Arguments:
- hidden_student: bfloat16 [4, 128, 2560], P('dp', 'section'), parts along dimension 0, may hold values from -8 to 8
- hidden_teacher: bfloat16 [4, 128, 4096], P('dp', 'section'), parts along dimension 0, may hold values from -8 to 8
- targets: int32 [4, 128], P('dp'), parts along dimension 0, may hold values from 0 to 81919
- w_student: bfloat16 [81920, 2560], P(('section', 'tensor')), may hold values from -4 to 4
- w_teacher: bfloat16 [81920, 4096], P(('section', 'tensor')), may hold values from -4 to 4
Outputs:
- loss: float32 [4], P('dp'), parts along dimension 0
- grad_hidden: bfloat16 [4, 128, 2560], P('dp', 'section', 'tensor'), parts along dimension 0
- grad_weight: bfloat16 [163840, 2560], P(('dp', 'section', 'tensor')), parts along dimension 0
The draws below stay inside these ranges and needn't reach their ends.
There are 2 independent parts, one for each index of `dp`. The reference program is written for one: setup_inputs(seed, part) draws one part's arguments, and reference() takes and returns one part's arrays. A program takes and returns all parts, laid end to end along the dimension named above; an argument that names none is the same for every part. Nothing has to cross between parts.
All inputs are finite; a program needn't handle non-finite values.
Results may differ from the reference program's by a relative error of at most 0.0048.
Values may be sent and summed in bfloat16 or wider, within the bound.
No kernel may reach another device: no remote copies, remote signals or barrier semaphores. Data moves between devices by JAX's collectives and lax.ppermute only.
A program may use at most 64 MiB of HBM per device.

```python
import math
import jax
import jax.numpy as jnp
from jax import lax

D_S = 2560
D_T = 4096
MB_TOK = 128
MICRO = 2
VOCAB = 81920


def pair_vocab(pair_index):
    return 2 * ((2 * pair_index + 1) * VOCAB // 16)


def mixed_values(key, count, width, scale_low, scale_high):
    normal_key = jax.random.fold_in(key, 0)
    scale_key = jax.random.fold_in(key, 2)
    normal_part = jnp.clip(jax.random.normal(normal_key, (count, width), jnp.float32), -4.0, 4.0)
    values = normal_part
    row_scale = jnp.exp(jax.random.uniform(scale_key, (count, 1), jnp.float32, math.log(scale_low), math.log(scale_high)))
    return values * row_scale


def hidden_rows(key, width, salt, scale_low, scale_high):
    row_key = jax.random.fold_in(key, 7)
    chosen_rows = jax.random.permutation(row_key, MICRO * MB_TOK)[:3]
    key = jax.random.fold_in(key, salt)
    count = MICRO * MB_TOK
    values = mixed_values(key, count, width, scale_low, scale_high)
    position = lax.broadcasted_iota(jnp.int32, (count, 1), 0)
    for pair_index in range(3):
        blended = values
        values = jnp.where(position == chosen_rows[pair_index], blended, values)
    return values.reshape(MICRO, MB_TOK, width).astype(jnp.bfloat16)


def head_rows(key, width, salt, scale_low, scale_high):
    key = jax.random.fold_in(key, salt)
    values = mixed_values(key, VOCAB, width, scale_low, scale_high)
    position = lax.broadcasted_iota(jnp.int32, (VOCAB, 1), 0)
    rising = 0.5 + position.astype(jnp.float32) / VOCAB
    values = values * (3.0 / math.sqrt(width)) * rising
    for pair_index in range(3):
        main_blend = values
        values = jnp.where(position == pair_vocab(pair_index), main_blend, values)
        twin_blend = values
        values = jnp.where(position == pair_vocab(pair_index) + 1, twin_blend, values)
    return values.astype(jnp.bfloat16)


def draw_hidden_student(key, part):
    return hidden_rows(key, D_S, 1, 1.0, 1.0)


def draw_hidden_teacher(key, part):
    return hidden_rows(key, D_T, 2, 1.0, 1.0)


def draw_w_student(key, part):
    return head_rows(key, D_S, 3, 1.0, 1.0)


def draw_w_teacher(key, part):
    return head_rows(key, D_T, 4, 1.0, 1.0)


def touch_ends(drawn, key, least, top_value):
    longest = drawn.shape.index(max(drawn.shape))
    spots = []
    for shift in (0, 1):
        where = [jax.random.randint(jax.random.fold_in(key, axis), (), 0, length) for axis, length in enumerate(drawn.shape)]
        where[longest] = (where[longest] + shift) % drawn.shape[longest]
        spots.append(tuple(where))
    return drawn.at[spots[0]].set(least).at[spots[1]].set(top_value)


def setup_inputs(seed: int = 0, part: int = 0) -> dict:
    streams_of = jax.random.split(jax.random.key(seed), 6)
    own_keys = jax.random.split(jax.random.fold_in(streams_of[5], part), 6)
    hidden_student = draw_hidden_student(jax.random.fold_in(jax.random.fold_in(streams_of[5], part), 71), part)
    hidden_teacher = draw_hidden_teacher(jax.random.fold_in(jax.random.fold_in(streams_of[5], part), 71), part)
    targets = touch_ends(jax.random.randint(own_keys[2], (MICRO, MB_TOK), 0, VOCAB), jax.random.fold_in(own_keys[2], 1), 0, VOCAB - 1).astype(jnp.int32)
    w_student = draw_w_student(jax.random.fold_in(streams_of[5], 71), part)
    w_teacher = draw_w_teacher(jax.random.fold_in(streams_of[5], 71), part)
    return dict(hidden_student=hidden_student, hidden_teacher=hidden_teacher, targets=targets, w_student=w_student, w_teacher=w_teacher)


reciprocal_heat = 0.5
heat_factor = 2.0
distill_mixing_factor = 0.5


def reference(hidden_student, hidden_teacher, targets, w_student, w_teacher):
    row_count = MICRO * MB_TOK
    student_flat = hidden_student.reshape(row_count, D_S)
    teacher_flat = hidden_teacher.reshape(row_count, D_T)
    pupil_raw_values = jnp.dot(student_flat, w_student.T, preferred_element_type=jnp.float32)
    mentor_raw_values = jnp.dot(teacher_flat, w_teacher.T, preferred_element_type=jnp.float32)
    pupil_top_value = jnp.max(pupil_raw_values, axis=1)
    mentor_top_value = jnp.max(mentor_raw_values, axis=1)
    student_exp = jnp.exp(pupil_raw_values - pupil_top_value[:, None])
    warmed_mentor_powers = jnp.exp((pupil_raw_values - pupil_top_value[:, None]) * reciprocal_heat)
    mentor_powers = jnp.exp((mentor_raw_values - mentor_top_value[:, None]) * reciprocal_heat)
    student_total = jnp.sum(student_exp, axis=1)
    warmed_mentor_partition = jnp.sum(warmed_mentor_powers, axis=1)
    mentor_partition = jnp.sum(mentor_powers, axis=1)
    mismatch_accrued = jnp.sum(mentor_powers * ((mentor_raw_values - pupil_raw_values) * reciprocal_heat), axis=1)
    flat_targets = targets.reshape(row_count).astype(jnp.int32)
    column_ids = lax.broadcasted_iota(jnp.int32, (1, VOCAB), 1)
    target_hit = column_ids == flat_targets[:, None]
    correct_class_value = jnp.sum(jnp.where(target_hit, pupil_raw_values, jnp.float32(0.0)), axis=1)
    pupil_partition_lognat = pupil_top_value + jnp.log(student_total)
    warmed_mentor_lognorm_value = pupil_top_value * reciprocal_heat + jnp.log(warmed_mentor_partition)
    mentor_partition_lognat = mentor_top_value * reciprocal_heat + jnp.log(mentor_partition)
    sample_penalty = distill_mixing_factor * heat_factor ** 2 * (mismatch_accrued / mentor_partition - mentor_partition_lognat + warmed_mentor_lognorm_value) + (1.0 - distill_mixing_factor) * (pupil_partition_lognat - correct_class_value)
    loss = jnp.mean(sample_penalty.reshape(MICRO, MB_TOK), axis=1)
    pupil_raw_slope = distill_mixing_factor * heat_factor * (warmed_mentor_powers / warmed_mentor_partition[:, None] - mentor_powers / mentor_partition[:, None])
    pupil_raw_slope = pupil_raw_slope + (1.0 - distill_mixing_factor) * (student_exp / student_total[:, None] - target_hit.astype(jnp.float32))
    pupil_raw_slope = pupil_raw_slope.astype(jnp.bfloat16)
    grad_hidden = jnp.dot(pupil_raw_slope, w_student, preferred_element_type=jnp.float32).astype(jnp.bfloat16)
    grad_weight = jnp.dot(pupil_raw_slope.T, student_flat, preferred_element_type=jnp.float32).astype(jnp.bfloat16)
    return loss, grad_hidden.reshape(MICRO, MB_TOK, D_S), grad_weight
```

```python
import jax
import jax.numpy as jnp
import numpy as np
from jax import lax
from jax.sharding import Mesh, PartitionSpec as P

RING_Y, PAIR_X, CORES, RING_Z = 4, 2, 2, 8
SIZES = {"y": RING_Y, "x": PAIR_X, "c": CORES, "z": RING_Z}
bf16, f32 = jnp.bfloat16, jnp.float32


def swap(value, axis, mask=1):
    return lax.ppermute(value, axis, [(i, i ^ mask) for i in range(SIZES[axis])])


def shift(value, axis, step):
    size = SIZES[axis]
    return lax.ppermute(value, axis, [(i, (i + step) % size) for i in range(size)])


def rotate(value, dim, start):
    size = value.shape[dim]
    return lax.dynamic_slice_in_dim(jnp.concatenate([value, value], dim), start, size, dim)


def to_relative(value, y, x, c):
    lead = value.shape[:-1]
    v = value.reshape(*lead, RING_Y, PAIR_X, CORES, -1)
    n = len(lead)
    v = rotate(rotate(rotate(v, n, y), n + 1, x), n + 2, c)
    return v.reshape(*lead, -1)


def to_canonical(value, y, x, c):
    return to_relative(value, lax.rem(RING_Y - y, RING_Y), x, c)


def gather_rows(block):
    half = block.shape[0] // 2
    from_prev = shift(block, "y", 1)
    from_next = shift(block, "y", 3)
    across = swap(block, "x")
    across_prev = shift(across, "y", 1)
    across_next = shift(across, "y", 3)
    far_a = shift(from_prev[:half], "y", 1)
    far_b = shift(from_next[half:], "y", 3)
    across_far_a = shift(across_prev[:half], "y", 1)
    across_far_b = shift(across_next[half:], "y", 3)
    far = jnp.concatenate([far_a, far_b], 0)
    across_far = jnp.concatenate([across_far_a, across_far_b], 0)
    mine = [block, across, from_next, across_next, far, across_far, from_prev, across_prev]
    out = []
    for piece in mine:
        out += [piece, swap(piece, "c")]
    return jnp.concatenate(out, 0)


def merge(parts):
    top = parts[0][0]
    for p in parts[1:]:
        top = jnp.maximum(top, p[0])
    total = parts[0][1] * jnp.exp(parts[0][0] - top)
    for p in parts[1:]:
        total = total + p[1] * jnp.exp(p[0] - top)
    return jnp.stack([top, total])


def exchange_totals(part):
    part = merge([part, swap(part, "c")])
    part = merge([part, swap(part, "x")])
    part = merge([part, shift(part, "y", 1), shift(part, "y", 3), shift(part, "y", 2)])
    part = merge([part, swap(part, "z", 1)])
    part = merge([part, swap(part, "z", 2)])
    part = merge([part, swap(part, "z", 4)])
    return part


def reduce_rows(partial, z):
    rows, width = partial.shape
    block = rows // 16
    q = partial.reshape(8, 2, block, width)
    q = q[:, 0] + swap(q[:, 1].astype(bf16), "c").astype(f32)
    q = q.reshape(RING_Y, 2, block, width)
    moved = [shift(q[d].astype(bf16), "y", d) for d in range(1, RING_Y)]
    r = q[0] + moved[0].astype(f32) + moved[1].astype(f32) + moved[2].astype(f32)
    s = r[0] + swap(r[1].astype(bf16), "x").astype(f32)
    s = s.reshape(block, RING_Z, width // RING_Z).transpose(1, 0, 2)
    s = s.reshape(2, 2, 2, block, width // RING_Z)
    pick = lambda v, dim, at: lax.dynamic_index_in_dim(v, at, dim, keepdims=False)
    z0, z1, z2 = z % 2, (z // 2) % 2, z // 4
    s = pick(s, 2, z0) + swap(pick(s, 2, 1 - z0), "z", 1)
    s = pick(s, 1, z1) + swap(pick(s, 1, 1 - z1), "z", 2)
    s = pick(s, 0, z2) + swap(pick(s, 0, 1 - z2), "z", 4)
    return s


def per_device(hidden_student, hidden_teacher, targets, w_student, w_teacher):
    y, x, c, z = (lax.axis_index(a) for a in ("y", "x", "c", "z"))
    micro, tokens, width_s = hidden_student.shape
    width_t = hidden_teacher.shape[2]
    vocab = w_student.shape[0]
    start = (((y * PAIR_X + x) * CORES + c) * RING_Z + z) * vocab
    rows = micro * tokens
    block = jnp.concatenate(
        [hidden_student.reshape(rows, width_s), hidden_teacher.reshape(rows, width_t)], 1
    )
    h = gather_rows(block)
    hs, ht = h[:, :width_s], h[:, width_s:]
    tgt = targets.reshape(micro, 16, tokens).transpose(1, 0, 2).reshape(1, -1)
    tgt = to_relative(tgt, y, x, c) - start
    dims = (((1,), (1,)), ((), ()))
    s = lax.dot_general(w_student, hs, dims, preferred_element_type=f32)
    t = lax.dot_general(w_teacher, ht, dims, preferred_element_type=f32)
    hit = lax.broadcasted_iota(jnp.int32, s.shape, 0) == tgt
    ms = jnp.max(s, axis=0, keepdims=True)
    mt = jnp.max(t, axis=0, keepdims=True)
    e2 = jnp.exp((s - ms) * 0.5)
    et = jnp.exp((t - mt) * 0.5)
    total = lambda v: jnp.sum(v, axis=0, keepdims=True)
    zero = jnp.zeros_like(ms)
    sums = [total(jnp.exp(s - ms)), total(e2), total(et), total(et * ((t - s) * 0.5))]
    sums += [total(jnp.where(hit, s, 0.0)), zero, zero, zero]
    tops = [ms, ms * 0.5, mt * 0.5, mt * 0.5, zero, zero, zero, zero]
    part = jnp.stack([jnp.concatenate(tops, 0), jnp.concatenate(sums, 0)])
    part = exchange_totals(to_canonical(part, y, x, c))
    part = to_relative(part, y, x, c)
    ms, half_mt = part[0, 0:1], part[0, 2:3]
    z1, z2, zt, cross, picked = (part[1, i : i + 1] for i in range(5))
    row_loss = 2.0 * (cross / zt - (half_mt + jnp.log(zt)) + (ms * 0.5 + jnp.log(z2))) + 0.5 * (
        ms + jnp.log(z1) - picked
    )
    loss = jnp.mean(row_loss.reshape(16, micro, tokens), axis=(0, 2))
    g = jnp.exp((s - ms) * 0.5) / z2 - jnp.exp(t * 0.5 - half_mt) / zt
    g = g + 0.5 * (jnp.exp(s - ms) / z1 - hit.astype(f32))
    g = g.astype(bf16)
    partial = lax.dot_general(g, w_student, (((0,), (0,)), ((), ())), preferred_element_type=f32)
    grad_hidden = reduce_rows(partial, z).astype(bf16).reshape(micro, tokens, -1)
    grad_weight = jnp.dot(g, hs, preferred_element_type=f32).astype(bf16)
    return loss, grad_hidden, grad_weight


def solution(mesh):
    sec = ("y", "x", "c")
    devices = np.asarray(mesh.devices).reshape(RING_Y, PAIR_X, CORES, RING_Z, -1)
    fine = Mesh(devices, sec + ("z", "dp"))
    return jax.shard_map(
        per_device,
        mesh=fine,
        in_specs=(
            P("dp", sec, None),
            P("dp", sec, None),
            P("dp", None),
            P(sec + ("z",), None),
            P(sec + ("z",), None),
        ),
        out_specs=(P("dp"), P("dp", sec, "z"), P(("dp",) + sec + ("z",), None)),
        check_vma=False,
    )
```

```python
import jax
import jax.numpy as jnp
import numpy as np
from jax import lax
from jax.experimental import pallas as pl
from jax.experimental.pallas import tpu as pltpu
from jax.sharding import Mesh, PartitionSpec as P

RING_Y, PAIR_X, CORES, RING_Z = 4, 2, 2, 8
SIZES = {"y": RING_Y, "x": PAIR_X, "c": CORES, "z": RING_Z}
MB = 1 << 20
bf16, f32 = jnp.bfloat16, jnp.float32
VMEM = pl.BlockSpec(memory_space=pltpu.VMEM)
SMEM = pl.BlockSpec(memory_space=pltpu.SMEM)


def swap(value, axis, mask=1):
    return lax.ppermute(value, axis, [(i, i ^ mask) for i in range(SIZES[axis])])


def shift(value, axis, step):
    size = SIZES[axis]
    return lax.ppermute(value, axis, [(i, (i + step) % size) for i in range(size)])


EARLY = ((0, 0), (0, 1), (1, 0), (3, 0))
LATE = ((2, 0), (2, 1), (1, 1), (3, 1))


def gather_rows(block):
    across = swap(block, "x")
    prev = shift(block, "y", 1)
    next_ = shift(block, "y", 3)
    prev_across = swap(prev, "x")
    next_across = swap(next_, "x")
    held, across = lax.optimization_barrier((block, across))
    far = shift(held, "y", 2)
    far_across = shift(across, "y", 2)
    early = [block, across, next_, prev]
    return early + [swap(piece, "c") for piece in early], (far, far_across, next_across, prev_across)


def first_entry(vocab):
    y, x, c, z = (lax.axis_index(a) for a in ("y", "x", "c", "z"))
    return (((y * PAIR_X + x) * CORES + c) * RING_Z + z) * vocab


def permuted(v, pick, back):
    dims = (((1,), (1,)), ((), ())) if back else (((1,), (0,)), ((), ()))
    out = None
    for _ in range(3):
        part = v.astype(bf16)
        v = v - part.astype(f32)
        moved = lax.dot_general(part, pick, dims, preferred_element_type=f32)
        out = moved if out is None else out + moved
    return out


def join_kernel(a_ref, b_ref, tgt_ref, out_ref, row_ref, pick_ref, sems):
    width = a_ref.shape[1]
    copies = [
        pltpu.make_async_copy(a_ref, out_ref.at[:, :width], sems.at[0]),
        pltpu.make_async_copy(b_ref, out_ref.at[:, width:], sems.at[1]),
    ]
    for copy in copies:
        copy.start()
    to = lax.broadcasted_iota(jnp.int32, (1, 256), 1)
    place = lax.rem(to // 16, 4) + to // 128 * 4
    dy, dx = jnp.zeros_like(to), jnp.zeros_like(to)
    for i, (v, w) in enumerate(EARLY + LATE):
        dy = jnp.where(place == i, v, dy)
        dx = jnp.where(place == i, w, dx)
    at_c = lax.rem(lax.rem(to // 64, CORES) + lax.axis_index("c"), CORES)
    at_y = lax.rem(dy + lax.axis_index("y"), RING_Y)
    at_x = lax.rem(dx + lax.axis_index("x"), PAIR_X)
    section = (at_y * PAIR_X + at_x) * CORES + at_c
    source = lax.rem(to // 8, 2) * 128 + section * 8 + lax.rem(to, 8)
    pick = lax.broadcasted_iota(jnp.int32, (256, 256), 0) == source
    pick = jnp.where(pick, 1.0, 0.0).astype(bf16)
    pick_ref[...] = pick
    tgt = jnp.concatenate([tgt_ref[0:1], tgt_ref[1:2]], 1).astype(f32)
    tgt = jnp.concatenate([tgt, jnp.zeros((7, 256), f32)], 0)
    row_ref[...] = permuted(tgt, pick, False)[0:1].astype(jnp.int32)
    for copy in copies:
        copy.wait()


def join(student, teacher, targets):
    rows = student.shape[0]
    width = student.shape[1] + teacher.shape[1]
    shape = jax.ShapeDtypeStruct
    return pl.pallas_call(
        join_kernel,
        out_shape=(
            shape((rows, width), bf16),
            shape((1, 256), jnp.int32),
            shape((256, 256), bf16),
        ),
        in_specs=[pl.BlockSpec(memory_space=pl.ANY)] * 2 + [VMEM],
        out_specs=(VMEM,) * 3,
        scratch_shapes=[pltpu.SemaphoreType.DMA((2,))],
        compiler_params=pltpu.CompilerParams(vmem_limit_bytes=4 * MB),
        name="join",
    )(student, teacher, targets)


def half_logits(blocks, ws_ref, wt_ref, tgt, s_ref, t_ref, hs_ref, ht_ref):
    width = ws_ref.shape[1]
    for i, ref in enumerate(blocks):
        hs_ref[i * 16 : i * 16 + 16, :] = ref[:, :width]
        ht_ref[i * 16 : i * 16 + 16, :] = ref[:, width:]
    dims = (((1,), (1,)), ((), ()))
    s = lax.dot_general(ws_ref[...], hs_ref[...], dims, preferred_element_type=f32)
    s_ref[...] = s
    ms = jnp.max(s, axis=0, keepdims=True)
    total = lambda v: jnp.sum(v, axis=0, keepdims=True)
    hit = lax.broadcasted_iota(jnp.int32, s.shape, 0) == tgt - first_entry(s.shape[0])
    z1 = total(jnp.exp(s - ms))
    z2 = total(jnp.exp((s - ms) * 0.5))
    picked = total(jnp.where(hit, s, 0.0))
    t = lax.dot_general(wt_ref[...], ht_ref[...], dims, preferred_element_type=f32)
    t_ref[...] = t
    mt = jnp.max(t, axis=0, keepdims=True)
    et = jnp.exp((t - mt) * 0.5)
    zt = total(et)
    cross = total(et * ((t - s_ref[...]) * 0.5))
    zero = jnp.zeros_like(ms)
    rows = [ms, ms * 0.5, mt * 0.5, mt * 0.5, zero, zero, zero, zero]
    return jnp.concatenate(rows + [z1, z2, zt, cross, picked, zero, zero, zero], 0)


def early_kernel(*refs):
    ws_ref, wt_ref, tgt_ref = refs[8:11]
    s_ref, t_ref, hs_ref, part_ref, ht_ref = refs[11:]
    tgt = tgt_ref[:, :128]
    part_ref[...] = half_logits(refs[:8], ws_ref, wt_ref, tgt, s_ref, t_ref, hs_ref, ht_ref)


def late_kernel(*refs):
    ws_ref, wt_ref, tgt_ref, early_ref, pick_ref = refs[8:13]
    s_ref, t_ref, hs_ref, part_ref, ht_ref = refs[13:]
    tgt = tgt_ref[:, 128:]
    part = half_logits(refs[:8], ws_ref, wt_ref, tgt, s_ref, t_ref, hs_ref, ht_ref)
    part = jnp.concatenate([early_ref[...], part], 1)
    part_ref[...] = permuted(part, pick_ref[...], True)


def compute_logits(blocks, ws, wt, tgt, extra=()):
    vocab, width = ws.shape
    rows = 128
    shape = jax.ShapeDtypeStruct
    return pl.pallas_call(
        late_kernel if extra else early_kernel,
        out_shape=(
            shape((vocab, rows), f32),
            shape((vocab, rows), f32),
            shape((rows, width), bf16),
            shape((16, 2 * rows if extra else rows), f32),
        ),
        in_specs=[VMEM] * (11 + len(extra)),
        out_specs=(VMEM,) * 4,
        scratch_shapes=[pltpu.VMEM((rows, wt.shape[1]), bf16)],
        compiler_params=pltpu.CompilerParams(vmem_limit_bytes=20 * MB),
        cost_estimate=pl.CostEstimate(
            flops=2 * vocab * rows * (width + wt.shape[1]),
            bytes_accessed=12 * MB,
            transcendentals=3 * vocab * rows,
        ),
        name="late_logits" if extra else "early_logits",
    )(*blocks, ws, wt, tgt, *extra)


def slope_kernel(*refs):
    s_refs, t_refs = refs[:2], refs[2:4]
    part_ref, pick_ref, tgt_ref, ws_ref, g_ref, send_ref, keep_ref, loss_ref = refs[4:]
    part = permuted(part_ref[...], pick_ref[...], False)
    first = first_entry(ws_ref.shape[0])
    ms, half_mt = part[0:1], part[2:3]
    z1, z2, zt, cross, picked = (part[8 + i : 9 + i] for i in range(5))
    loss = 2.0 * (cross / zt - (half_mt + jnp.log(zt)) + (ms * 0.5 + jnp.log(z2)))
    loss = loss + 0.5 * (ms + jnp.log(z1) - picked)
    micro = lax.rem(lax.broadcasted_iota(jnp.int32, loss.shape, 1) // 8, 2)
    for i in range(2):
        loss_ref[i] = jnp.sum(jnp.where(micro == i, loss, 0.0)) * (1.0 / 128.0)
    tgt = tgt_ref[...] - first
    r2, rt, r1 = 1.0 / z2, 1.0 / zt, 0.5 / z1
    for i in range(2):
        at = slice(i * 128, i * 128 + 128)
        d = s_refs[i][...] - ms[:, at]
        hit = lax.broadcasted_iota(jnp.int32, d.shape, 0) == tgt[:, at]
        g = jnp.exp(d * 0.5) * r2[:, at]
        g = g - jnp.exp(t_refs[i][...] * 0.5 - half_mt[:, at]) * rt[:, at]
        g = g + (jnp.exp(d) * r1[:, at] - jnp.where(hit, 0.5, 0.0))
        g_ref[:, at] = g.astype(bf16)
    p = lax.dot_general(
        g_ref[...], ws_ref[...], (((0,), (0,)), ((), ())), preferred_element_type=f32
    )
    for i, (dy, dx) in enumerate(EARLY + LATE):
        out = slice((dy * PAIR_X + dx) * 16, (dy * PAIR_X + dx) * 16 + 16)
        row = i // 4 * 128 + i % 4 * 16
        keep_ref[out] = p[row : row + 16]
        send_ref[out] = p[row + 64 : row + 80].astype(bf16)


def compute_slope(s, t, part, pick, tgt, ws):
    vocab, width = ws.shape
    rows = 256
    shape = jax.ShapeDtypeStruct
    return pl.pallas_call(
        slope_kernel,
        out_shape=(
            shape((vocab, rows), bf16),
            shape((rows // 2, width), bf16),
            shape((rows // 2, width), f32),
            shape((2,), f32),
        ),
        in_specs=[VMEM] * 8,
        out_specs=(VMEM,) * 3 + (SMEM,),
        compiler_params=pltpu.CompilerParams(vmem_limit_bytes=20 * MB),
        cost_estimate=pl.CostEstimate(
            flops=2 * vocab * rows * width, bytes_accessed=8 * MB, transcendentals=3 * vocab * rows
        ),
        name="slope",
    )(*s, *t, part, pick, tgt, ws)


def weight_kernel(g_ref, a_ref, b_ref, out_ref, done_ref):
    h = jnp.concatenate([a_ref[...], b_ref[...]], 0)
    out_ref[...] = jnp.dot(g_ref[...], h, preferred_element_type=f32).astype(bf16)
    done_ref[...] = jnp.zeros(done_ref.shape, f32)


def compute_weight(g, early, late):
    vocab, rows = g.shape
    width = early.shape[1]
    tile = 128
    shape = jax.ShapeDtypeStruct
    return pl.pallas_call(
        weight_kernel,
        out_shape=(shape((vocab, width), bf16), shape((8, 128), f32)),
        grid=(vocab // tile,),
        in_specs=[
            pl.BlockSpec((tile, rows), lambda i: (i, 0)),
            pl.BlockSpec((rows // 2, width), lambda i: (0, 0)),
            pl.BlockSpec((rows // 2, width), lambda i: (0, 0)),
        ],
        out_specs=(
            pl.BlockSpec((tile, width), lambda i: (i, 0)),
            pl.BlockSpec((8, 128), lambda i: (0, 0)),
        ),
        compiler_params=pltpu.CompilerParams(vmem_limit_bytes=12 * MB),
        cost_estimate=pl.CostEstimate(
            flops=2 * vocab * rows * width, bytes_accessed=6 * MB, transcendentals=0
        ),
        name="weight",
    )(g, early, late)


def split_kernel(own_ref, got_ref, ahead_ref, behind_ref, keep_ref, tmp_ref):
    z = lax.axis_index("z")
    width = own_ref.shape[1] // RING_Z
    v = own_ref[...] + got_ref[...].astype(f32)
    for k in range(RING_Z):
        tmp_ref[k] = v[:, k * width : (k + 1) * width]
    at = lambda d: tmp_ref[lax.rem(z + (d + RING_Z), RING_Z)]
    for i, d in enumerate((2, 3, 4)):
        ahead_ref[i] = at(d)
    for i, d in enumerate((-3, -2)):
        behind_ref[i] = at(d)
    for i, d in enumerate((-1, 0, 1)):
        keep_ref[i] = at(d)


def split_features(own, got):
    rows, width = own.shape
    shape = lambda n: jax.ShapeDtypeStruct((n, rows, width // RING_Z), f32)
    return pl.pallas_call(
        split_kernel,
        out_shape=(shape(3), shape(2), shape(3)),
        in_specs=[VMEM, VMEM],
        out_specs=(VMEM,) * 3,
        scratch_shapes=[pltpu.VMEM((RING_Z, rows, width // RING_Z), f32)],
        compiler_params=pltpu.CompilerParams(vmem_limit_bytes=4 * MB),
        name="split",
    )(own, got)


def merge(parts):
    tops = [p[:8] for p in parts]
    top = tops[0]
    for v in tops[1:]:
        top = jnp.maximum(top, v)
    total = parts[0][8:] * jnp.exp(tops[0] - top)
    for v, p in zip(tops[1:], parts[1:]):
        total = total + p[8:] * jnp.exp(v - top)
    return jnp.concatenate([top, total], 0)


def exchange_totals(part):
    part = merge([part, swap(part, "c")])
    part = merge([part, swap(part, "x")])
    part = merge([part, shift(part, "y", 1), shift(part, "y", 3), shift(part, "y", 2)])
    prev, next_ = shift(part, "z", 1), shift(part, "z", 7)
    two, three = merge([part, prev]), merge([part, prev, next_])
    return merge([three, shift(three, "z", 3), shift(two, "z", 5)])


def core_kernel(keep_ref, got_ref, own_ref, *out_refs):
    rows = own_ref.shape[0]
    own_ref[...] = keep_ref[:rows] + got_ref[:rows].astype(f32)
    for i, ref in enumerate(out_refs):
        at = slice((i + 1) * rows, (i + 2) * rows)
        ref[...] = (keep_ref[at] + got_ref[at].astype(f32)).astype(bf16)


def add_core(keep, got):
    rows, width = keep.shape
    rows = rows // RING_Y
    shape = jax.ShapeDtypeStruct
    return pl.pallas_call(
        core_kernel,
        out_shape=(shape((rows, width), f32),) + (shape((rows, width), bf16),) * 3,
        in_specs=[VMEM] * 2,
        out_specs=(VMEM,) * 4,
        compiler_params=pltpu.CompilerParams(vmem_limit_bytes=8 * MB),
        name="add_core",
    )(keep, got)


def ring_kernel(own_ref, a_ref, b_ref, c_ref, after_ref, keep_ref, send_ref):
    rows = keep_ref.shape[0]
    for i, ref in enumerate((keep_ref, send_ref)):
        at = slice(i * rows, (i + 1) * rows)
        total = own_ref[at] + a_ref[at].astype(f32)
        total = total + b_ref[at].astype(f32) + c_ref[at].astype(f32)
        ref[...] = total.astype(ref.dtype)


def add_ring(own, moved, after):
    rows, width = own.shape
    rows = rows // PAIR_X
    shape = jax.ShapeDtypeStruct
    return pl.pallas_call(
        ring_kernel,
        out_shape=(shape((rows, width), f32), shape((rows, width), bf16)),
        in_specs=[VMEM] * 5,
        out_specs=(VMEM,) * 2,
        compiler_params=pltpu.CompilerParams(vmem_limit_bytes=6 * MB),
        name="add_ring",
    )(own, *moved, after)


def reduce_rows(send, keep, after):
    own, *parts = add_core(keep, swap(send, "c"))
    moved = [shift(part, "y", d + 1) for d, part in enumerate(parts)]
    own, part = add_ring(own, moved, after)
    ahead, behind, mine = split_features(own, swap(part, "x"))
    from_a, from_b = shift(ahead, "z", 3), shift(behind, "z", 5)
    to_next = mine[2] + from_a[2] + from_b[1]
    to_prev = mine[0] + from_a[0]
    own = mine[1] + from_a[1] + from_b[0]
    return own + shift(to_next, "z", 1) + shift(to_prev, "z", 7)


def per_device(hidden_student, hidden_teacher, targets, w_student, w_teacher):
    micro, tokens, _ = hidden_student.shape
    rows = micro * tokens
    block, tgt, pick = join(
        hidden_student.reshape(rows, -1), hidden_teacher.reshape(rows, -1), targets
    )
    early, late = gather_rows(block)
    s_early, t_early, h_early, part = compute_logits(early, w_student, w_teacher, tgt)
    late, part = lax.optimization_barrier((late, part))
    late = list(late) + [swap(piece, "c") for piece in late]
    s_late, t_late, h_late, part = compute_logits(late, w_student, w_teacher, tgt, (part, pick))
    part = exchange_totals(part)
    s, t = (s_early, s_late), (t_early, t_late)
    g, send, keep, loss = compute_slope(s, t, part, pick, tgt, w_student)
    grad_weight, done = compute_weight(g, h_early, h_late)
    grad_hidden = reduce_rows(send, keep, done)
    return loss, grad_hidden.astype(bf16).reshape(micro, tokens, -1), grad_weight


def solution(mesh):
    sec = ("y", "x", "c")
    devices = np.asarray(mesh.devices).reshape(RING_Y, PAIR_X, CORES, RING_Z, -1)
    fine = Mesh(devices, sec + ("z", "dp"))
    return jax.shard_map(
        per_device,
        mesh=fine,
        in_specs=(
            P("dp", sec, None),
            P("dp", sec, None),
            P("dp", None),
            P(sec + ("z",), None),
            P(sec + ("z",), None),
        ),
        out_specs=(P("dp"), P("dp", sec, "z"), P(("dp",) + sec + ("z",), None)),
        check_vma=False,
    )
```

```python
import functools

import jax
import jax.numpy as jnp
import numpy as np
from jax import lax
from jax.experimental import pallas as pl
from jax.experimental.pallas import tpu as pltpu
from jax.sharding import Mesh, PartitionSpec as P

RING_Y, PAIR_X, CORES, RING_Z = 4, 2, 2, 8
SIZES = {"y": RING_Y, "x": PAIR_X, "c": CORES, "z": RING_Z}
MB = 1 << 20
JOIN_MB = 4
bf16, f32 = jnp.bfloat16, jnp.float32
VMEM = pl.BlockSpec(memory_space=pltpu.VMEM)
SMEM = pl.BlockSpec(memory_space=pltpu.SMEM)


def swap(value, axis, mask=1):
    return lax.ppermute(value, axis, [(i, i ^ mask) for i in range(SIZES[axis])])


def shift(value, axis, step):
    size = SIZES[axis]
    return lax.ppermute(value, axis, [(i, (i + step) % size) for i in range(size)])


EARLY = ((0, 0), (0, 1), (3, 0), (1, 0))
LATE = ((3, 1), (1, 1), (2, 0), (2, 1))


def gather_rows(block):
    across = swap(block, "x")
    prev = shift(block, "y", 1)
    next_ = shift(block, "y", 3)
    sides, here = pair(prev, next_), pair(block, across)
    early = here, swap(here, "c"), sides, swap(sides, "c")
    return early, (swap(sides, "x"), shift(here, "y", 2))


def first_entry(vocab):
    y, x, c, z = (lax.axis_index(a) for a in ("y", "x", "c", "z"))
    return (((y * PAIR_X + x) * CORES + c) * RING_Z + z) * vocab


def permuted(v, pick, back):
    dims = (((1,), (1,)), ((), ())) if back else (((1,), (0,)), ((), ()))
    out = None
    for _ in range(3):
        part = v.astype(bf16)
        v = v - part.astype(f32)
        moved = lax.dot_general(part, pick, dims, preferred_element_type=f32)
        out = moved if out is None else out + moved
    return out


def join_kernel(a_ref, b_ref, out_ref):
    width = a_ref.shape[1]
    out_ref[:, :width] = a_ref[...]
    out_ref[:, width:] = b_ref[...]


def join(student, teacher):
    rows = student.shape[0]
    return pl.pallas_call(
        join_kernel,
        out_shape=jax.ShapeDtypeStruct((rows, student.shape[1] + teacher.shape[1]), bf16),
        in_specs=[VMEM] * 2,
        out_specs=VMEM,
        compiler_params=pltpu.CompilerParams(vmem_limit_bytes=JOIN_MB * MB),
        name="join",
    )(student, teacher)


def pair_kernel(a_ref, b_ref, out_ref):
    rows = a_ref.shape[0]
    out_ref[:rows] = a_ref[...]
    out_ref[rows:] = b_ref[...]


def pair(a, b):
    return pl.pallas_call(
        pair_kernel,
        out_shape=jax.ShapeDtypeStruct((2 * a.shape[0], a.shape[1]), bf16),
        in_specs=[VMEM] * 2,
        out_specs=VMEM,
        compiler_params=pltpu.CompilerParams(vmem_limit_bytes=2 * MB),
        name="pair",
    )(a, b)


def rows_kernel(tgt_ref, row_ref, pick_ref):
    to = lax.broadcasted_iota(jnp.int32, (1, 256), 1)
    place = to // 128 * 4 + lax.rem(to // 64, 2) * 2 + lax.rem(to // 16, 2)
    dc = lax.rem(to // 32, CORES)
    dy, dx = jnp.zeros_like(to), jnp.zeros_like(to)
    for i, (v, w) in enumerate(EARLY + LATE):
        dy = jnp.where(place == i, v, dy)
        dx = jnp.where(place == i, w, dx)
    at_c = lax.rem(dc + lax.axis_index("c"), CORES)
    at_y = lax.rem(dy + lax.axis_index("y"), RING_Y)
    at_x = lax.rem(dx + lax.axis_index("x"), PAIR_X)
    section = (at_y * PAIR_X + at_x) * CORES + at_c
    source = lax.rem(to // 8, 2) * 128 + section * 8 + lax.rem(to, 8)
    pick = lax.broadcasted_iota(jnp.int32, (256, 256), 0) == source
    pick = jnp.where(pick, 1.0, 0.0).astype(bf16)
    pick_ref[...] = pick
    tgt = jnp.concatenate([tgt_ref[0:1], tgt_ref[1:2]], 1).astype(f32)
    tgt = jnp.concatenate([tgt, jnp.zeros((7, 256), f32)], 0)
    row_ref[...] = permuted(tgt, pick, False)[0:1].astype(jnp.int32)


def row_order(targets):
    shape = jax.ShapeDtypeStruct
    return pl.pallas_call(
        rows_kernel,
        out_shape=(shape((1, 256), jnp.int32), shape((256, 256), bf16)),
        in_specs=[VMEM],
        out_specs=(VMEM,) * 2,
        compiler_params=pltpu.CompilerParams(vmem_limit_bytes=2 * MB),
        name="row_order",
    )(targets)


def half_logits(blocks, ws_ref, wt_ref, tgt, s_ref, t_ref, hs_ref, ht_ref):
    width = ws_ref.shape[1]
    for i, ref in enumerate(blocks):
        hs_ref[i * 32 : i * 32 + 32, :] = ref[:, :width]
        ht_ref[i * 32 : i * 32 + 32, :] = ref[:, width:]
    dims = (((1,), (1,)), ((), ()))
    s = lax.dot_general(ws_ref[...], hs_ref[...], dims, preferred_element_type=f32)
    s_ref[...] = s
    ms = jnp.max(s, axis=0, keepdims=True)
    total = lambda v: jnp.sum(v, axis=0, keepdims=True)
    hit = lax.broadcasted_iota(jnp.int32, s.shape, 0) == tgt - first_entry(s.shape[0])
    z1 = total(jnp.exp(s - ms))
    z2 = total(jnp.exp((s - ms) * 0.5))
    picked = total(jnp.where(hit, s, 0.0))
    t = lax.dot_general(wt_ref[...], ht_ref[...], dims, preferred_element_type=f32)
    t_ref[...] = t
    mt = jnp.max(t, axis=0, keepdims=True)
    et = jnp.exp((t - mt) * 0.5)
    zt = total(et)
    cross = total(et * ((t - s_ref[...]) * 0.5))
    zero = jnp.zeros_like(ms)
    rows = [ms, ms * 0.5, mt * 0.5, mt * 0.5, zero, zero, zero, zero]
    return jnp.concatenate(rows + [z1, z2, zt, cross, picked, zero, zero, zero], 0)


def early_kernel(*refs):
    ws_ref, wt_ref, tgt_ref = refs[4:7]
    s_ref, t_ref, hs_ref, part_ref, ht_ref = refs[7:]
    tgt = tgt_ref[:, :128]
    part_ref[...] = half_logits(refs[:4], ws_ref, wt_ref, tgt, s_ref, t_ref, hs_ref, ht_ref)


def late_kernel(*refs):
    ws_ref, wt_ref, tgt_ref, early_ref, pick_ref = refs[4:9]
    s_ref, t_ref, hs_ref, part_ref, ht_ref = refs[9:]
    tgt = tgt_ref[:, 128:]
    part = half_logits(refs[:4], ws_ref, wt_ref, tgt, s_ref, t_ref, hs_ref, ht_ref)
    part = jnp.concatenate([early_ref[...], part], 1)
    part_ref[...] = permuted(part, pick_ref[...], True)


def compute_logits(blocks, ws, wt, tgt, extra=()):
    vocab, width = ws.shape
    rows = 128
    shape = jax.ShapeDtypeStruct
    return pl.pallas_call(
        late_kernel if extra else early_kernel,
        out_shape=(
            shape((vocab, rows), f32),
            shape((vocab, rows), f32),
            shape((rows, width), bf16),
            shape((16, 2 * rows if extra else rows), f32),
        ),
        in_specs=[VMEM] * (7 + len(extra)),
        out_specs=(VMEM,) * 4,
        scratch_shapes=[pltpu.VMEM((rows, wt.shape[1]), bf16)],
        compiler_params=pltpu.CompilerParams(vmem_limit_bytes=20 * MB),
        cost_estimate=pl.CostEstimate(
            flops=2 * vocab * rows * (width + wt.shape[1]),
            bytes_accessed=12 * MB,
            transcendentals=3 * vocab * rows,
        ),
        name="late_logits" if extra else "early_logits",
    )(*blocks, ws, wt, tgt, *extra)


def slope_kernel(*refs):
    s_refs, t_refs = refs[:2], refs[2:4]
    pick_ref, tgt_ref, ws_ref, g_ref, send_ref, keep_ref, loss_ref = refs[7:]
    part = permuted(merge([ref[...] for ref in refs[4:7]]), pick_ref[...], False)
    first = first_entry(ws_ref.shape[0])
    ms, half_mt = part[0:1], part[2:3]
    z1, z2, zt, cross, picked = (part[8 + i : 9 + i] for i in range(5))
    loss = 2.0 * (cross / zt - (half_mt + jnp.log(zt)) + (ms * 0.5 + jnp.log(z2)))
    loss = loss + 0.5 * (ms + jnp.log(z1) - picked)
    micro = lax.rem(lax.broadcasted_iota(jnp.int32, loss.shape, 1) // 8, 2)
    for i in range(2):
        loss_ref[i] = jnp.sum(jnp.where(micro == i, loss, 0.0)) * (1.0 / 128.0)
    tgt = tgt_ref[...] - first
    r2, rt, r1 = 1.0 / z2, 1.0 / zt, 0.5 / z1
    for i in range(2):
        at = slice(i * 128, i * 128 + 128)
        d = s_refs[i][...] - ms[:, at]
        hit = lax.broadcasted_iota(jnp.int32, d.shape, 0) == tgt[:, at]
        g = jnp.exp(d * 0.5) * r2[:, at]
        g = g - jnp.exp(t_refs[i][...] * 0.5 - half_mt[:, at]) * rt[:, at]
        g = g + (jnp.exp(d) * r1[:, at] - jnp.where(hit, 0.5, 0.0))
        g_ref[:, at] = g.astype(bf16)
    p = lax.dot_general(
        g_ref[...], ws_ref[...], (((0,), (0,)), ((), ())), preferred_element_type=f32
    )
    for i, (dy, dx) in enumerate(EARLY + LATE):
        out = slice((dy * PAIR_X + dx) * 16, (dy * PAIR_X + dx) * 16 + 16)
        row = i // 2 * 64 + i % 2 * 16
        keep_ref[out] = p[row : row + 16]
        send_ref[out] = p[row + 32 : row + 48].astype(bf16)


def compute_slope(s, t, parts, pick, tgt, ws):
    vocab, width = ws.shape
    rows = 256
    shape = jax.ShapeDtypeStruct
    return pl.pallas_call(
        slope_kernel,
        out_shape=(
            shape((vocab, rows), bf16),
            shape((rows // 2, width), bf16),
            shape((rows // 2, width), f32),
            shape((2,), f32),
        ),
        in_specs=[VMEM] * 10,
        out_specs=(VMEM,) * 3 + (SMEM,),
        compiler_params=pltpu.CompilerParams(vmem_limit_bytes=20 * MB),
        cost_estimate=pl.CostEstimate(
            flops=2 * vocab * rows * width, bytes_accessed=8 * MB, transcendentals=3 * vocab * rows
        ),
        name="slope",
    )(*s, *t, *parts, pick, tgt, ws)


def weight_kernel(g_ref, a_ref, b_ref, out_ref, done_ref):
    h = jnp.concatenate([a_ref[...], b_ref[...]], 0)
    out_ref[...] = jnp.dot(g_ref[...], h, preferred_element_type=f32).astype(bf16)
    done_ref[...] = jnp.zeros(done_ref.shape, f32)


def compute_weight(g, early, late):
    vocab, rows = g.shape
    width = early.shape[1]
    tile = 128
    shape = jax.ShapeDtypeStruct
    return pl.pallas_call(
        weight_kernel,
        out_shape=(shape((vocab, width), bf16), shape((8, 128), f32)),
        grid=(vocab // tile,),
        in_specs=[
            pl.BlockSpec((tile, rows), lambda i: (i, 0)),
            pl.BlockSpec((rows // 2, width), lambda i: (0, 0)),
            pl.BlockSpec((rows // 2, width), lambda i: (0, 0)),
        ],
        out_specs=(
            pl.BlockSpec((tile, width), lambda i: (i, 0)),
            pl.BlockSpec((8, 128), lambda i: (0, 0)),
        ),
        compiler_params=pltpu.CompilerParams(vmem_limit_bytes=12 * MB),
        cost_estimate=pl.CostEstimate(
            flops=2 * vocab * rows * width, bytes_accessed=6 * MB, transcendentals=0
        ),
        name="weight",
    )(g, early, late)


def split_kernel(own_ref, got_ref, ahead_ref, behind_ref, keep_ref, tmp_ref):
    z = lax.axis_index("z")
    width = own_ref.shape[1] // RING_Z
    v = own_ref[...] + got_ref[...].astype(f32)
    for k in range(RING_Z):
        tmp_ref[k] = v[:, k * width : (k + 1) * width]
    at = lambda d: tmp_ref[lax.rem(z + (d + RING_Z), RING_Z)]
    for i, d in enumerate((2, 3, 4)):
        ahead_ref[i] = at(d)
    for i, d in enumerate((-2, -3)):
        behind_ref[i] = at(d)
    for i, d in enumerate((-1, 0, 1)):
        keep_ref[i] = at(d)


def split_features(own, got):
    rows, width = own.shape
    shape = lambda n: jax.ShapeDtypeStruct((n, rows, width // RING_Z), f32)
    return pl.pallas_call(
        split_kernel,
        out_shape=(shape(3), shape(2), shape(3)),
        in_specs=[VMEM, VMEM],
        out_specs=(VMEM,) * 3,
        scratch_shapes=[pltpu.VMEM((RING_Z, rows, width // RING_Z), f32)],
        compiler_params=pltpu.CompilerParams(vmem_limit_bytes=4 * MB),
        name="split",
    )(own, got)


def merge(parts):
    tops = [p[:8] for p in parts]
    top = tops[0]
    for v in tops[1:]:
        top = jnp.maximum(top, v)
    total = parts[0][8:] * jnp.exp(tops[0] - top)
    for v, p in zip(tops[1:], parts[1:]):
        total = total + p[8:] * jnp.exp(v - top)
    return jnp.concatenate([top, total], 0)


def merge_kernel(*refs, sizes):
    for size, ref in zip(sizes, refs[-len(sizes) :]):
        ref[...] = merge([v[...] for v in refs[:size]])


def merged(parts, sizes):
    shape = jax.ShapeDtypeStruct(parts[0].shape, f32)
    return pl.pallas_call(
        functools.partial(merge_kernel, sizes=sizes),
        out_shape=(shape,) * len(sizes),
        in_specs=[VMEM] * len(parts),
        out_specs=(VMEM,) * len(sizes),
        compiler_params=pltpu.CompilerParams(vmem_limit_bytes=2 * MB),
        name="merge",
    )(*parts)


def exchange_totals(part):
    (part,) = merged([part, swap(part, "c")], (2,))
    (part,) = merged([part, swap(part, "x")], (2,))
    parts = [part, shift(part, "y", 1), shift(part, "y", 3), shift(part, "y", 2)]
    (part,) = merged(parts, (4,))
    two, three = merged([part, shift(part, "z", 1), shift(part, "z", 7)], (2, 3))
    return three, shift(three, "z", 5), shift(two, "z", 2)


def core_kernel(keep_ref, got_ref, own_ref, *out_refs):
    rows = own_ref.shape[0]
    own_ref[...] = keep_ref[:rows] + got_ref[:rows].astype(f32)
    for i, ref in enumerate(out_refs):
        at = slice((i + 1) * rows, (i + 2) * rows)
        ref[...] = (keep_ref[at] + got_ref[at].astype(f32)).astype(bf16)


def add_core(keep, got):
    rows, width = keep.shape
    rows = rows // RING_Y
    shape = jax.ShapeDtypeStruct
    return pl.pallas_call(
        core_kernel,
        out_shape=(shape((rows, width), f32),) + (shape((rows, width), bf16),) * 3,
        in_specs=[VMEM] * 2,
        out_specs=(VMEM,) * 4,
        compiler_params=pltpu.CompilerParams(vmem_limit_bytes=8 * MB),
        name="add_core",
    )(keep, got)


def ring_kernel(own_ref, a_ref, b_ref, c_ref, after_ref, keep_ref, send_ref):
    rows = keep_ref.shape[0]
    for i, ref in enumerate((keep_ref, send_ref)):
        at = slice(i * rows, (i + 1) * rows)
        total = own_ref[at] + a_ref[at].astype(f32)
        total = total + b_ref[at].astype(f32) + c_ref[at].astype(f32)
        ref[...] = total.astype(ref.dtype)


def add_ring(own, moved, after):
    rows, width = own.shape
    rows = rows // PAIR_X
    shape = jax.ShapeDtypeStruct
    return pl.pallas_call(
        ring_kernel,
        out_shape=(shape((rows, width), f32), shape((rows, width), bf16)),
        in_specs=[VMEM] * 5,
        out_specs=(VMEM,) * 2,
        compiler_params=pltpu.CompilerParams(vmem_limit_bytes=6 * MB),
        name="add_ring",
    )(own, *moved, after)


def reduce_rows(send, keep, after):
    own, *parts = add_core(keep, swap(send, "c"))
    moved = [shift(part, "y", d + 1) for d, part in enumerate(parts)]
    own, part = add_ring(own, moved, after)
    ahead, behind, mine = split_features(own, swap(part, "x"))
    from_a, from_b = shift(ahead, "z", 3), shift(behind, "z", 6)
    to_next = mine[2] + from_a[2]
    to_prev = mine[0] + from_a[0] + from_b[1]
    own = mine[1] + from_a[1] + from_b[0]
    return own + shift(to_next, "z", 1) + shift(to_prev, "z", 7)


def per_device(hidden_student, hidden_teacher, targets, w_student, w_teacher):
    micro, tokens, _ = hidden_student.shape
    rows = micro * tokens
    block = join(hidden_student.reshape(rows, -1), hidden_teacher.reshape(rows, -1))
    tgt, pick = row_order(targets)
    early, (sides, far) = gather_rows(block)
    s_early, t_early, h_early, part = compute_logits(early, w_student, w_teacher, tgt)
    far, part = lax.optimization_barrier((far, part))
    late = sides, swap(sides, "c"), far, swap(far, "c")
    s_late, t_late, h_late, part = compute_logits(late, w_student, w_teacher, tgt, (part, pick))
    parts = exchange_totals(part)
    s, t = (s_early, s_late), (t_early, t_late)
    g, send, keep, loss = compute_slope(s, t, parts, pick, tgt, w_student)
    grad_weight, done = compute_weight(g, h_early, h_late)
    grad_hidden = reduce_rows(send, keep, done)
    return loss, grad_hidden.astype(bf16).reshape(micro, tokens, -1), grad_weight


def solution(mesh):
    sec = ("y", "x", "c")
    devices = np.asarray(mesh.devices).reshape(RING_Y, PAIR_X, CORES, RING_Z, -1)
    fine = Mesh(devices, sec + ("z", "dp"))
    return jax.shard_map(
        per_device,
        mesh=fine,
        in_specs=(
            P("dp", sec, None),
            P("dp", sec, None),
            P("dp", None),
            P(sec + ("z",), None),
            P(sec + ("z",), None),
        ),
        out_specs=(P("dp"), P("dp", sec, "z"), P(("dp",) + sec + ("z",), None)),
        check_vma=False,
    )
```

```python
import functools

import jax
import jax.numpy as jnp
import numpy as np
from jax import lax
from jax.experimental import pallas as pl
from jax.experimental.pallas import tpu as pltpu
from jax.sharding import Mesh, PartitionSpec as P

RING_Y, PAIR_X, CORES, RING_Z = 4, 2, 2, 8
SIZES = {"y": RING_Y, "x": PAIR_X, "c": CORES, "z": RING_Z}
MB = 1 << 20
bf16, f32 = jnp.bfloat16, jnp.float32
VMEM = pl.BlockSpec(memory_space=pltpu.VMEM)
SMEM = pl.BlockSpec(memory_space=pltpu.SMEM)


def swap(value, axis, mask=1):
    return lax.ppermute(value, axis, [(i, i ^ mask) for i in range(SIZES[axis])])


def shift(value, axis, step):
    size = SIZES[axis]
    return lax.ppermute(value, axis, [(i, (i + step) % size) for i in range(size)])


EARLY = ((0, 0), (0, 1), (3, 0), (1, 0))
LATE = ((3, 1), (1, 1), (2, 0), (2, 1))


def gather_rows(block, tgt):
    across = swap(block, "x")
    prev = shift(block, "y", 1)
    next_ = shift(block, "y", 3)
    sides, here = pair(prev, next_), pair(block, across)
    held, tgt = lax.optimization_barrier((here, tgt))
    early = here, swap(held, "c"), sides, swap(sides, "c")
    return early, (swap(sides, "x"), shift(here, "y", 2)), tgt


def first_entry(vocab):
    y, x, c, z = (lax.axis_index(a) for a in ("y", "x", "c", "z"))
    return (((y * PAIR_X + x) * CORES + c) * RING_Z + z) * vocab


def permuted(v, pick, back):
    dims = (((1,), (1,)), ((), ())) if back else (((1,), (0,)), ((), ()))
    out = None
    for _ in range(3):
        part = v.astype(bf16)
        v = v - part.astype(f32)
        moved = lax.dot_general(part, pick, dims, preferred_element_type=f32)
        out = moved if out is None else out + moved
    return out


def join_kernel(a_ref, b_ref, out_ref):
    width = a_ref.shape[1]
    out_ref[:, :width] = a_ref[...]
    out_ref[:, width:] = b_ref[...]


def join(student, teacher):
    rows = student.shape[0]
    return pl.pallas_call(
        join_kernel,
        out_shape=jax.ShapeDtypeStruct((rows, student.shape[1] + teacher.shape[1]), bf16),
        in_specs=[VMEM] * 2,
        out_specs=VMEM,
        compiler_params=pltpu.CompilerParams(vmem_limit_bytes=4 * MB),
        name="join",
    )(student, teacher)


def pair_kernel(a_ref, b_ref, out_ref):
    rows = a_ref.shape[0]
    out_ref[:rows] = a_ref[...]
    out_ref[rows:] = b_ref[...]


def pair(a, b):
    return pl.pallas_call(
        pair_kernel,
        out_shape=jax.ShapeDtypeStruct((2 * a.shape[0], a.shape[1]), bf16),
        in_specs=[VMEM] * 2,
        out_specs=VMEM,
        compiler_params=pltpu.CompilerParams(vmem_limit_bytes=2 * MB),
        name="pair",
    )(a, b)


def rows_kernel(tgt_ref, row_ref, pick_ref):
    to = lax.broadcasted_iota(jnp.int32, (1, 256), 1)
    place = to // 128 * 4 + lax.rem(to // 64, 2) * 2 + lax.rem(to // 16, 2)
    dc = lax.rem(to // 32, CORES)
    dy, dx = jnp.zeros_like(to), jnp.zeros_like(to)
    for i, (v, w) in enumerate(EARLY + LATE):
        dy = jnp.where(place == i, v, dy)
        dx = jnp.where(place == i, w, dx)
    at_c = lax.rem(dc + lax.axis_index("c"), CORES)
    at_y = lax.rem(dy + lax.axis_index("y"), RING_Y)
    at_x = lax.rem(dx + lax.axis_index("x"), PAIR_X)
    section = (at_y * PAIR_X + at_x) * CORES + at_c
    source = lax.rem(to // 8, 2) * 128 + section * 8 + lax.rem(to, 8)
    pick = lax.broadcasted_iota(jnp.int32, (256, 256), 0) == source
    pick = jnp.where(pick, 1.0, 0.0).astype(bf16)
    pick_ref[...] = pick
    tgt = jnp.concatenate([tgt_ref[0:1], tgt_ref[1:2]], 1).astype(f32)
    tgt = jnp.concatenate([tgt, jnp.zeros((7, 256), f32)], 0)
    row_ref[...] = permuted(tgt, pick, False)[0:1].astype(jnp.int32)


def row_order(targets):
    shape = jax.ShapeDtypeStruct
    return pl.pallas_call(
        rows_kernel,
        out_shape=(shape((1, 256), jnp.int32), shape((256, 256), bf16)),
        in_specs=[VMEM],
        out_specs=(VMEM,) * 2,
        compiler_params=pltpu.CompilerParams(vmem_limit_bytes=2 * MB),
        name="row_order",
    )(targets)


def half_logits(blocks, ws_ref, wt_ref, tgt, s_ref, t_ref, hs_ref):
    width = ws_ref.shape[1]
    for i, ref in enumerate(blocks):
        hs_ref[i * 32 : i * 32 + 32, :] = ref[:, :width]
    ht = jnp.concatenate([ref[:, width:] for ref in blocks], 0)
    dims = (((1,), (1,)), ((), ()))
    s = lax.dot_general(ws_ref[...], hs_ref[...], dims, preferred_element_type=f32)
    s_ref[...] = s
    ms = jnp.max(s, axis=0, keepdims=True)
    total = lambda v: jnp.sum(v, axis=0, keepdims=True)
    hit = lax.broadcasted_iota(jnp.int32, s.shape, 0) == tgt - first_entry(s.shape[0])
    root = jnp.exp((s - ms) * 0.5)
    z1 = total(root * root)
    z2 = total(root)
    picked = total(jnp.where(hit, s, 0.0))
    t = lax.dot_general(wt_ref[...], ht, dims, preferred_element_type=f32)
    t_ref[...] = t
    mt = jnp.max(t, axis=0, keepdims=True)
    et = jnp.exp((t - mt) * 0.5)
    zt = total(et)
    cross = total(et * ((t - s_ref[...]) * 0.5))
    zero = jnp.zeros_like(ms)
    rows = [ms, ms * 0.5, mt * 0.5, mt * 0.5, zero, zero, zero, zero]
    return jnp.concatenate(rows + [z1, z2, zt, cross, picked, zero, zero, zero], 0)


def early_kernel(*refs):
    ws_ref, wt_ref, tgt_ref = refs[4:7]
    s_ref, t_ref, hs_ref, part_ref = refs[7:]
    tgt = tgt_ref[:, :128]
    part_ref[...] = half_logits(refs[:4], ws_ref, wt_ref, tgt, s_ref, t_ref, hs_ref)


def late_kernel(*refs):
    ws_ref, wt_ref, tgt_ref, early_ref, pick_ref = refs[4:9]
    s_ref, t_ref, hs_ref, part_ref = refs[9:]
    tgt = tgt_ref[:, 128:]
    part = half_logits(refs[:4], ws_ref, wt_ref, tgt, s_ref, t_ref, hs_ref)
    part = jnp.concatenate([early_ref[...], part], 1)
    part_ref[...] = permuted(part, pick_ref[...], True)


def compute_logits(blocks, ws, wt, tgt, extra=()):
    vocab, width = ws.shape
    rows = 128
    shape = jax.ShapeDtypeStruct
    return pl.pallas_call(
        late_kernel if extra else early_kernel,
        out_shape=(
            shape((vocab, rows), f32),
            shape((vocab, rows), f32),
            shape((rows, width), bf16),
            shape((16, 2 * rows if extra else rows), f32),
        ),
        in_specs=[VMEM] * (7 + len(extra)),
        out_specs=(VMEM,) * 4,
        compiler_params=pltpu.CompilerParams(vmem_limit_bytes=20 * MB),
        cost_estimate=pl.CostEstimate(
            flops=2 * vocab * rows * (width + wt.shape[1]),
            bytes_accessed=12 * MB,
            transcendentals=3 * vocab * rows,
        ),
        name="late_logits" if extra else "early_logits",
    )(*blocks, ws, wt, tgt, *extra)


def slope_kernel(*refs):
    s_refs, t_refs = refs[:2], refs[2:4]
    pick_ref, tgt_ref, ws_ref, g_ref, send_ref, keep_ref, loss_ref = refs[7:]
    part = permuted(merge([ref[...] for ref in refs[4:7]]), pick_ref[...], False)
    first = first_entry(ws_ref.shape[0])
    ms, half_mt = part[0:1], part[2:3]
    z1, z2, zt, cross, picked = (part[8 + i : 9 + i] for i in range(5))
    loss = 2.0 * (cross / zt - (half_mt + jnp.log(zt)) + (ms * 0.5 + jnp.log(z2)))
    loss = loss + 0.5 * (ms + jnp.log(z1) - picked)
    micro = lax.rem(lax.broadcasted_iota(jnp.int32, loss.shape, 1) // 8, 2)
    for i in range(2):
        loss_ref[i] = jnp.sum(jnp.where(micro == i, loss, 0.0)) * (1.0 / 128.0)
    tgt = tgt_ref[...] - first
    r2, rt, r1 = 1.0 / z2, 1.0 / zt, 0.5 / z1
    for i in range(2):
        at = slice(i * 128, i * 128 + 128)
        d = s_refs[i][...] - ms[:, at]
        hit = lax.broadcasted_iota(jnp.int32, d.shape, 0) == tgt[:, at]
        root = jnp.exp(d * 0.5)
        g = root * r2[:, at]
        g = g - jnp.exp(t_refs[i][...] * 0.5 - half_mt[:, at]) * rt[:, at]
        g = g + (root * root * r1[:, at] - jnp.where(hit, 0.5, 0.0))
        g_ref[:, at] = g.astype(bf16)
    p = lax.dot_general(
        g_ref[...], ws_ref[...], (((0,), (0,)), ((), ())), preferred_element_type=f32
    )
    for i, (dy, dx) in enumerate(EARLY + LATE):
        out = slice((dy * PAIR_X + dx) * 16, (dy * PAIR_X + dx) * 16 + 16)
        row = i // 2 * 64 + i % 2 * 16
        keep_ref[out] = p[row : row + 16]
        send_ref[out] = p[row + 32 : row + 48].astype(bf16)


def compute_slope(s, t, parts, pick, tgt, ws):
    vocab, width = ws.shape
    rows = 256
    shape = jax.ShapeDtypeStruct
    return pl.pallas_call(
        slope_kernel,
        out_shape=(
            shape((vocab, rows), bf16),
            shape((rows // 2, width), bf16),
            shape((rows // 2, width), f32),
            shape((2,), f32),
        ),
        in_specs=[VMEM] * 10,
        out_specs=(VMEM,) * 3 + (SMEM,),
        compiler_params=pltpu.CompilerParams(vmem_limit_bytes=20 * MB),
        cost_estimate=pl.CostEstimate(
            flops=2 * vocab * rows * width, bytes_accessed=8 * MB, transcendentals=3 * vocab * rows
        ),
        name="slope",
    )(*s, *t, *parts, pick, tgt, ws)


def weight_kernel(g_ref, a_ref, b_ref, out_ref, done_ref):
    h = jnp.concatenate([a_ref[...], b_ref[...]], 0)
    out_ref[...] = jnp.dot(g_ref[...], h, preferred_element_type=f32).astype(bf16)
    done_ref[...] = jnp.zeros(done_ref.shape, f32)


def compute_weight(g, early, late):
    vocab, rows = g.shape
    width = early.shape[1]
    tile = 128
    shape = jax.ShapeDtypeStruct
    return pl.pallas_call(
        weight_kernel,
        out_shape=(shape((vocab, width), bf16), shape((8, 128), f32)),
        grid=(vocab // tile,),
        in_specs=[
            pl.BlockSpec((tile, rows), lambda i: (i, 0)),
            pl.BlockSpec((rows // 2, width), lambda i: (0, 0)),
            pl.BlockSpec((rows // 2, width), lambda i: (0, 0)),
        ],
        out_specs=(
            pl.BlockSpec((tile, width), lambda i: (i, 0)),
            pl.BlockSpec((8, 128), lambda i: (0, 0)),
        ),
        compiler_params=pltpu.CompilerParams(vmem_limit_bytes=12 * MB),
        cost_estimate=pl.CostEstimate(
            flops=2 * vocab * rows * width, bytes_accessed=6 * MB, transcendentals=0
        ),
        name="weight",
    )(g, early, late)


def split_kernel(own_ref, got_ref, ahead_ref, behind_ref, keep_ref, tmp_ref):
    z = lax.axis_index("z")
    width = own_ref.shape[1] // RING_Z
    v = own_ref[...] + got_ref[...].astype(f32)
    for k in range(RING_Z):
        tmp_ref[k] = v[:, k * width : (k + 1) * width]
    at = lambda d: tmp_ref[lax.rem(z + (d + RING_Z), RING_Z)]
    for i, d in enumerate((2, 3, 4)):
        ahead_ref[i] = at(d)
    for i, d in enumerate((-2, -3)):
        behind_ref[i] = at(d)
    for i, d in enumerate((-1, 0, 1)):
        keep_ref[i] = at(d)


def split_features(own, got):
    rows, width = own.shape
    shape = lambda n: jax.ShapeDtypeStruct((n, rows, width // RING_Z), f32)
    return pl.pallas_call(
        split_kernel,
        out_shape=(shape(3), shape(2), shape(3)),
        in_specs=[VMEM, VMEM],
        out_specs=(VMEM,) * 3,
        scratch_shapes=[pltpu.VMEM((RING_Z, rows, width // RING_Z), f32)],
        compiler_params=pltpu.CompilerParams(vmem_limit_bytes=4 * MB),
        name="split",
    )(own, got)


def merge(parts):
    tops = [p[:8] for p in parts]
    top = tops[0]
    for v in tops[1:]:
        top = jnp.maximum(top, v)
    total = parts[0][8:] * jnp.exp(tops[0] - top)
    for v, p in zip(tops[1:], parts[1:]):
        total = total + p[8:] * jnp.exp(v - top)
    return jnp.concatenate([top, total], 0)


def merge_kernel(*refs, sizes):
    for size, ref in zip(sizes, refs[-len(sizes) :]):
        ref[...] = merge([v[...] for v in refs[:size]])


def merged(parts, sizes):
    shape = jax.ShapeDtypeStruct(parts[0].shape, f32)
    return pl.pallas_call(
        functools.partial(merge_kernel, sizes=sizes),
        out_shape=(shape,) * len(sizes),
        in_specs=[VMEM] * len(parts),
        out_specs=(VMEM,) * len(sizes),
        compiler_params=pltpu.CompilerParams(vmem_limit_bytes=2 * MB),
        name="merge",
    )(*parts)


def exchange_totals(part):
    (part,) = merged([part, swap(part, "c")], (2,))
    (part,) = merged([part, swap(part, "x")], (2,))
    parts = [part, shift(part, "y", 1), shift(part, "y", 3), shift(part, "y", 2)]
    (part,) = merged(parts, (4,))
    two, three = merged([part, shift(part, "z", 1), shift(part, "z", 7)], (2, 3))
    return three, shift(three, "z", 5), shift(two, "z", 2)


def core_kernel(keep_ref, got_ref, own_ref, *out_refs):
    rows = own_ref.shape[0]
    own_ref[...] = keep_ref[:rows] + got_ref[:rows].astype(f32)
    for i, ref in enumerate(out_refs):
        at = slice((i + 1) * rows, (i + 2) * rows)
        ref[...] = (keep_ref[at] + got_ref[at].astype(f32)).astype(bf16)


def add_core(keep, got):
    rows, width = keep.shape
    rows = rows // RING_Y
    shape = jax.ShapeDtypeStruct
    return pl.pallas_call(
        core_kernel,
        out_shape=(shape((rows, width), f32),) + (shape((rows, width), bf16),) * 3,
        in_specs=[VMEM] * 2,
        out_specs=(VMEM,) * 4,
        compiler_params=pltpu.CompilerParams(vmem_limit_bytes=8 * MB),
        name="add_core",
    )(keep, got)


def ring_kernel(own_ref, a_ref, b_ref, c_ref, after_ref, keep_ref, send_ref):
    rows = keep_ref.shape[0]
    for i, ref in enumerate((keep_ref, send_ref)):
        at = slice(i * rows, (i + 1) * rows)
        total = own_ref[at] + a_ref[at].astype(f32)
        total = total + b_ref[at].astype(f32) + c_ref[at].astype(f32)
        ref[...] = total.astype(ref.dtype)


def add_ring(own, moved, after):
    rows, width = own.shape
    rows = rows // PAIR_X
    shape = jax.ShapeDtypeStruct
    return pl.pallas_call(
        ring_kernel,
        out_shape=(shape((rows, width), f32), shape((rows, width), bf16)),
        in_specs=[VMEM] * 5,
        out_specs=(VMEM,) * 2,
        compiler_params=pltpu.CompilerParams(vmem_limit_bytes=6 * MB),
        name="add_ring",
    )(own, *moved, after)


def far_kernel(mine_ref, a_ref, b_ref, next_ref, prev_ref, own_ref):
    next_ref[...] = mine_ref[2] + a_ref[2]
    prev_ref[...] = mine_ref[0] + a_ref[0] + b_ref[1]
    own_ref[...] = mine_ref[1] + a_ref[1] + b_ref[0]


def add_far(mine, from_a, from_b):
    return pl.pallas_call(
        far_kernel,
        out_shape=(jax.ShapeDtypeStruct(mine.shape[1:], f32),) * 3,
        in_specs=[VMEM] * 3,
        out_specs=(VMEM,) * 3,
        compiler_params=pltpu.CompilerParams(vmem_limit_bytes=2 * MB),
        name="add_far",
    )(mine, from_a, from_b)


def reduce_rows(send, keep, after):
    own, *parts = add_core(keep, swap(send, "c"))
    moved = [shift(part, "y", d + 1) for d, part in enumerate(parts)]
    own, part = add_ring(own, moved, after)
    ahead, behind, mine = split_features(own, swap(part, "x"))
    from_a, from_b = shift(ahead, "z", 3), shift(behind, "z", 6)
    to_next, to_prev, own = add_far(mine, from_a, from_b)
    return own + shift(to_next, "z", 1) + shift(to_prev, "z", 7)


def per_device(hidden_student, hidden_teacher, targets, w_student, w_teacher):
    micro, tokens, _ = hidden_student.shape
    rows = micro * tokens
    block = join(hidden_student.reshape(rows, -1), hidden_teacher.reshape(rows, -1))
    tgt, pick = row_order(targets)
    early, (sides, far), tgt = gather_rows(block, tgt)
    s_early, t_early, h_early, part = compute_logits(early, w_student, w_teacher, tgt)
    sides, part = lax.optimization_barrier((sides, part))
    sides_swapped = swap(sides, "c")
    far, sides_swapped = lax.optimization_barrier((far, sides_swapped))
    late = sides, sides_swapped, far, swap(far, "c")
    s_late, t_late, h_late, part = compute_logits(late, w_student, w_teacher, tgt, (part, pick))
    parts = exchange_totals(part)
    s, t = (s_early, s_late), (t_early, t_late)
    g, send, keep, loss = compute_slope(s, t, parts, pick, tgt, w_student)
    grad_weight, done = compute_weight(g, h_early, h_late)
    grad_hidden = reduce_rows(send, keep, done)
    return loss, grad_hidden.astype(bf16).reshape(micro, tokens, -1), grad_weight


def solution(mesh):
    sec = ("y", "x", "c")
    devices = np.asarray(mesh.devices).reshape(RING_Y, PAIR_X, CORES, RING_Z, -1)
    fine = Mesh(devices, sec + ("z", "dp"))
    return jax.shard_map(
        per_device,
        mesh=fine,
        in_specs=(
            P("dp", sec, None),
            P("dp", sec, None),
            P("dp", None),
            P(sec + ("z",), None),
            P(sec + ("z",), None),
        ),
        out_specs=(P("dp"), P("dp", sec, "z"), P(("dp",) + sec + ("z",), None)),
        check_vma=False,
    )
```

```python
import functools

import jax
import jax.numpy as jnp
import numpy as np
from jax import lax
from jax.experimental import pallas as pl
from jax.experimental.pallas import tpu as pltpu
from jax.sharding import Mesh, PartitionSpec as P

RING_Y, PAIR_X, CORES, RING_Z = 4, 2, 2, 8
SIZES = {"y": RING_Y, "x": PAIR_X, "c": CORES, "z": RING_Z}
MB = 1 << 20
bf16, f32 = jnp.bfloat16, jnp.float32
VMEM = pl.BlockSpec(memory_space=pltpu.VMEM)
SMEM = pl.BlockSpec(memory_space=pltpu.SMEM)


def swap(value, axis, mask=1):
    return lax.ppermute(value, axis, [(i, i ^ mask) for i in range(SIZES[axis])])


def shift(value, axis, step):
    size = SIZES[axis]
    return lax.ppermute(value, axis, [(i, (i + step) % size) for i in range(size)])


EARLY = ((0, 0), (0, 1), (3, 0), (1, 0))
LATE = ((3, 1), (1, 1), (2, 0), (2, 1))


def gather_rows(block, tgt):
    across = swap(block, "x")
    prev = shift(block, "y", 1)
    next_ = shift(block, "y", 3)
    sides, here = pair(prev, next_), pair(block, across)
    held, tgt = lax.optimization_barrier((here, tgt))
    early = here, swap(held, "c"), sides, swap(sides, "c")
    return early, (swap(sides, "x"), shift(here, "y", 2)), tgt


def first_entry(vocab):
    y, x, c, z = (lax.axis_index(a) for a in ("y", "x", "c", "z"))
    return (((y * PAIR_X + x) * CORES + c) * RING_Z + z) * vocab


def permuted(v, pick, back):
    dims = (((1,), (1,)), ((), ())) if back else (((1,), (0,)), ((), ()))
    out = None
    for _ in range(3):
        part = v.astype(bf16)
        v = v - part.astype(f32)
        moved = lax.dot_general(part, pick, dims, preferred_element_type=f32)
        out = moved if out is None else out + moved
    return out


def join_kernel(a_ref, b_ref, out_ref):
    width = a_ref.shape[1]
    out_ref[:, :width] = a_ref[...]
    out_ref[:, width:] = b_ref[...]


def join(student, teacher):
    rows = student.shape[0]
    return pl.pallas_call(
        join_kernel,
        out_shape=jax.ShapeDtypeStruct((rows, student.shape[1] + teacher.shape[1]), bf16),
        in_specs=[VMEM] * 2,
        out_specs=VMEM,
        compiler_params=pltpu.CompilerParams(vmem_limit_bytes=4 * MB),
        name="join",
    )(student, teacher)


def pair_kernel(a_ref, b_ref, out_ref):
    rows = a_ref.shape[0]
    out_ref[:rows] = a_ref[...]
    out_ref[rows:] = b_ref[...]


def pair(a, b):
    return pl.pallas_call(
        pair_kernel,
        out_shape=jax.ShapeDtypeStruct((2 * a.shape[0], a.shape[1]), bf16),
        in_specs=[VMEM] * 2,
        out_specs=VMEM,
        compiler_params=pltpu.CompilerParams(vmem_limit_bytes=2 * MB),
        name="pair",
    )(a, b)


def rows_kernel(tgt_ref, row_ref, pick_ref):
    to = lax.broadcasted_iota(jnp.int32, (1, 256), 1)
    place = to // 128 * 4 + lax.rem(to // 64, 2) * 2 + lax.rem(to // 16, 2)
    dc = lax.rem(to // 32, CORES)
    dy, dx = jnp.zeros_like(to), jnp.zeros_like(to)
    for i, (v, w) in enumerate(EARLY + LATE):
        dy = jnp.where(place == i, v, dy)
        dx = jnp.where(place == i, w, dx)
    at_c = lax.rem(dc + lax.axis_index("c"), CORES)
    at_y = lax.rem(dy + lax.axis_index("y"), RING_Y)
    at_x = lax.rem(dx + lax.axis_index("x"), PAIR_X)
    section = (at_y * PAIR_X + at_x) * CORES + at_c
    source = lax.rem(to // 8, 2) * 128 + section * 8 + lax.rem(to, 8)
    pick = lax.broadcasted_iota(jnp.int32, (256, 256), 0) == source
    pick = jnp.where(pick, 1.0, 0.0).astype(bf16)
    pick_ref[...] = pick
    tgt = jnp.concatenate([tgt_ref[0:1], tgt_ref[1:2]], 1).astype(f32)
    tgt = jnp.concatenate([tgt, jnp.zeros((7, 256), f32)], 0)
    row_ref[...] = permuted(tgt, pick, False)[0:1].astype(jnp.int32)


def row_order(targets):
    shape = jax.ShapeDtypeStruct
    return pl.pallas_call(
        rows_kernel,
        out_shape=(shape((1, 256), jnp.int32), shape((256, 256), bf16)),
        in_specs=[VMEM],
        out_specs=(VMEM,) * 2,
        compiler_params=pltpu.CompilerParams(vmem_limit_bytes=2 * MB),
        name="row_order",
    )(targets)


def half_logits(blocks, ws_ref, wt_ref, tgt, s_ref, t_ref, hs_ref):
    width = ws_ref.shape[1]
    for i, ref in enumerate(blocks):
        hs_ref[i * 32 : i * 32 + 32, :] = ref[:, :width]
    ht = jnp.concatenate([ref[:, width:] for ref in blocks], 0)
    dims = (((1,), (1,)), ((), ()))
    s = lax.dot_general(ws_ref[...], hs_ref[...], dims, preferred_element_type=f32)
    s_ref[...] = s
    ms = jnp.max(s, axis=0, keepdims=True)
    total = lambda v: jnp.sum(v, axis=0, keepdims=True)
    hit = lax.broadcasted_iota(jnp.int32, s.shape, 0) == tgt - first_entry(s.shape[0])
    root = jnp.exp((s - ms) * 0.5)
    z1 = total(root * root)
    z2 = total(root)
    picked = total(jnp.where(hit, s, 0.0))
    t = lax.dot_general(wt_ref[...], ht, dims, preferred_element_type=f32)
    t_ref[...] = t
    mt = jnp.max(t, axis=0, keepdims=True)
    et = jnp.exp((t - mt) * 0.5)
    zt = total(et)
    cross = total(et * ((t - s_ref[...]) * 0.5))
    zero = jnp.zeros_like(ms)
    rows = [ms, ms * 0.5, mt * 0.5, mt * 0.5, zero, zero, zero, zero]
    return jnp.concatenate(rows + [z1, z2, zt, cross, picked, zero, zero, zero], 0)


def early_kernel(*refs):
    ws_ref, wt_ref, tgt_ref = refs[4:7]
    s_ref, t_ref, hs_ref, part_ref = refs[7:]
    tgt = tgt_ref[:, :128]
    part_ref[...] = half_logits(refs[:4], ws_ref, wt_ref, tgt, s_ref, t_ref, hs_ref)


def late_kernel(*refs):
    ws_ref, wt_ref, tgt_ref, early_ref, pick_ref = refs[4:9]
    s_ref, t_ref, hs_ref, part_ref = refs[9:]
    tgt = tgt_ref[:, 128:]
    part = half_logits(refs[:4], ws_ref, wt_ref, tgt, s_ref, t_ref, hs_ref)
    part = jnp.concatenate([early_ref[...], part], 1)
    part_ref[...] = permuted(part, pick_ref[...], True)


def compute_logits(blocks, ws, wt, tgt, extra=()):
    vocab, width = ws.shape
    rows = 128
    shape = jax.ShapeDtypeStruct
    return pl.pallas_call(
        late_kernel if extra else early_kernel,
        out_shape=(
            shape((vocab, rows), f32),
            shape((vocab, rows), f32),
            shape((rows, width), bf16),
            shape((16, 2 * rows if extra else rows), f32),
        ),
        in_specs=[VMEM] * (7 + len(extra)),
        out_specs=(VMEM,) * 4,
        compiler_params=pltpu.CompilerParams(vmem_limit_bytes=20 * MB),
        cost_estimate=pl.CostEstimate(
            flops=2 * vocab * rows * (width + wt.shape[1]),
            bytes_accessed=12 * MB,
            transcendentals=3 * vocab * rows,
        ),
        name="late_logits" if extra else "early_logits",
    )(*blocks, ws, wt, tgt, *extra)


def slope_kernel(*refs):
    s_refs, t_refs = refs[:2], refs[2:4]
    pick_ref, tgt_ref, ws_ref, g_ref, send_ref, keep_ref, loss_ref = refs[7:]
    part = permuted(merge([ref[...] for ref in refs[4:7]]), pick_ref[...], False)
    first = first_entry(ws_ref.shape[0])
    ms, half_mt = part[0:1], part[2:3]
    z1, z2, zt, cross, picked = (part[8 + i : 9 + i] for i in range(5))
    loss = 2.0 * (cross / zt - (half_mt + jnp.log(zt)) + (ms * 0.5 + jnp.log(z2)))
    loss = loss + 0.5 * (ms + jnp.log(z1) - picked)
    micro = lax.rem(lax.broadcasted_iota(jnp.int32, loss.shape, 1) // 8, 2)
    for i in range(2):
        loss_ref[i] = jnp.sum(jnp.where(micro == i, loss, 0.0)) * (1.0 / 128.0)
    tgt = tgt_ref[...] - first
    r2, rt, r1 = 1.0 / z2, 1.0 / zt, 0.5 / z1
    for i in range(2):
        at = slice(i * 128, i * 128 + 128)
        d = s_refs[i][...] - ms[:, at]
        hit = lax.broadcasted_iota(jnp.int32, d.shape, 0) == tgt[:, at]
        root = jnp.exp(d * 0.5)
        g = root * r2[:, at]
        g = g - jnp.exp(t_refs[i][...] * 0.5 - half_mt[:, at]) * rt[:, at]
        g = g + (root * root * r1[:, at] - jnp.where(hit, 0.5, 0.0))
        g_ref[:, at] = g.astype(bf16)
    p = lax.dot_general(
        g_ref[...], ws_ref[...], (((0,), (0,)), ((), ())), preferred_element_type=f32
    )
    for i, (dy, dx) in enumerate(EARLY + LATE):
        out = slice((dy * PAIR_X + dx) * 16, (dy * PAIR_X + dx) * 16 + 16)
        row = i // 2 * 64 + i % 2 * 16
        keep_ref[out] = p[row : row + 16]
        send_ref[out] = p[row + 32 : row + 48].astype(bf16)


def compute_slope(s, t, parts, pick, tgt, ws):
    vocab, width = ws.shape
    rows = 256
    shape = jax.ShapeDtypeStruct
    return pl.pallas_call(
        slope_kernel,
        out_shape=(
            shape((vocab, rows), bf16),
            shape((rows // 2, width), bf16),
            shape((rows // 2, width), f32),
            shape((2,), f32),
        ),
        in_specs=[VMEM] * 10,
        out_specs=(VMEM,) * 3 + (SMEM,),
        compiler_params=pltpu.CompilerParams(vmem_limit_bytes=20 * MB),
        cost_estimate=pl.CostEstimate(
            flops=2 * vocab * rows * width, bytes_accessed=8 * MB, transcendentals=3 * vocab * rows
        ),
        name="slope",
    )(*s, *t, *parts, pick, tgt, ws)


def weight_kernel(g_ref, a_ref, b_ref, out_ref, done_ref):
    h = jnp.concatenate([a_ref[...], b_ref[...]], 0)
    out_ref[...] = jnp.dot(g_ref[...], h, preferred_element_type=f32).astype(bf16)
    done_ref[...] = jnp.zeros(done_ref.shape, f32)


def compute_weight(g, early, late):
    vocab, rows = g.shape
    width = early.shape[1]
    tile = 128
    shape = jax.ShapeDtypeStruct
    return pl.pallas_call(
        weight_kernel,
        out_shape=(shape((vocab, width), bf16), shape((8, 128), f32)),
        grid=(vocab // tile,),
        in_specs=[
            pl.BlockSpec((tile, rows), lambda i: (i, 0)),
            pl.BlockSpec((rows // 2, width), lambda i: (0, 0)),
            pl.BlockSpec((rows // 2, width), lambda i: (0, 0)),
        ],
        out_specs=(
            pl.BlockSpec((tile, width), lambda i: (i, 0)),
            pl.BlockSpec((8, 128), lambda i: (0, 0)),
        ),
        compiler_params=pltpu.CompilerParams(vmem_limit_bytes=12 * MB),
        cost_estimate=pl.CostEstimate(
            flops=2 * vocab * rows * width, bytes_accessed=6 * MB, transcendentals=0
        ),
        name="weight",
    )(g, early, late)


def split_kernel(own_ref, got_ref, ahead_ref, behind_ref, keep_ref, tmp_ref):
    z = lax.axis_index("z")
    width = own_ref.shape[1] // RING_Z
    v = own_ref[...] + got_ref[...].astype(f32)
    for k in range(RING_Z):
        tmp_ref[k] = v[:, k * width : (k + 1) * width]
    at = lambda d: tmp_ref[lax.rem(z + (d + RING_Z), RING_Z)]
    for i, d in enumerate((2, 3, 4)):
        ahead_ref[i] = at(d)
    for i, d in enumerate((-2, -3)):
        behind_ref[i] = at(d)
    for i, d in enumerate((-1, 0, 1)):
        keep_ref[i] = at(d)


def split_features(own, got):
    rows, width = own.shape
    shape = lambda n: jax.ShapeDtypeStruct((n, rows, width // RING_Z), f32)
    return pl.pallas_call(
        split_kernel,
        out_shape=(shape(3), shape(2), shape(3)),
        in_specs=[VMEM, VMEM],
        out_specs=(VMEM,) * 3,
        scratch_shapes=[pltpu.VMEM((RING_Z, rows, width // RING_Z), f32)],
        compiler_params=pltpu.CompilerParams(vmem_limit_bytes=4 * MB),
        name="split",
    )(own, got)


def merge(parts):
    tops = [p[:8] for p in parts]
    top = tops[0]
    for v in tops[1:]:
        top = jnp.maximum(top, v)
    total = parts[0][8:] * jnp.exp(tops[0] - top)
    for v, p in zip(tops[1:], parts[1:]):
        total = total + p[8:] * jnp.exp(v - top)
    return jnp.concatenate([top, total], 0)


def merge_kernel(*refs, sizes):
    for size, ref in zip(sizes, refs[-len(sizes) :]):
        ref[...] = merge([v[...] for v in refs[:size]])


def merged(parts, sizes):
    shape = jax.ShapeDtypeStruct(parts[0].shape, f32)
    return pl.pallas_call(
        functools.partial(merge_kernel, sizes=sizes),
        out_shape=(shape,) * len(sizes),
        in_specs=[VMEM] * len(parts),
        out_specs=(VMEM,) * len(sizes),
        compiler_params=pltpu.CompilerParams(vmem_limit_bytes=2 * MB),
        name="merge",
    )(*parts)


def exchange_totals(part):
    (part,) = merged([part, swap(part, "c")], (2,))
    (part,) = merged([part, swap(part, "x")], (2,))
    parts = [part, shift(part, "y", 1), shift(part, "y", 3), shift(part, "y", 2)]
    (part,) = merged(parts, (4,))
    two, three = merged([part, shift(part, "z", 1), shift(part, "z", 7)], (2, 3))
    return three, shift(three, "z", 5), shift(two, "z", 2)


def core_kernel(keep_ref, got_ref, own_ref, *out_refs):
    rows = own_ref.shape[0]
    own_ref[...] = keep_ref[:rows] + got_ref[:rows].astype(f32)
    for i, ref in enumerate(out_refs):
        at = slice((i + 1) * rows, (i + 2) * rows)
        ref[...] = (keep_ref[at] + got_ref[at].astype(f32)).astype(bf16)


def add_core(keep, got):
    rows, width = keep.shape
    rows = rows // RING_Y
    shape = jax.ShapeDtypeStruct
    return pl.pallas_call(
        core_kernel,
        out_shape=(shape((rows, width), f32),) + (shape((rows, width), bf16),) * 3,
        in_specs=[VMEM] * 2,
        out_specs=(VMEM,) * 4,
        compiler_params=pltpu.CompilerParams(vmem_limit_bytes=8 * MB),
        name="add_core",
    )(keep, got)


def ring_kernel(own_ref, a_ref, b_ref, c_ref, after_ref, keep_ref, send_ref):
    rows = keep_ref.shape[0]
    for i, ref in enumerate((keep_ref, send_ref)):
        at = slice(i * rows, (i + 1) * rows)
        total = own_ref[at] + a_ref[at].astype(f32)
        total = total + b_ref[at].astype(f32) + c_ref[at].astype(f32)
        ref[...] = total.astype(ref.dtype)


def add_ring(own, moved, after):
    rows, width = own.shape
    rows = rows // PAIR_X
    shape = jax.ShapeDtypeStruct
    return pl.pallas_call(
        ring_kernel,
        out_shape=(shape((rows, width), f32), shape((rows, width), bf16)),
        in_specs=[VMEM] * 5,
        out_specs=(VMEM,) * 2,
        compiler_params=pltpu.CompilerParams(vmem_limit_bytes=6 * MB),
        name="add_ring",
    )(own, *moved, after)


def far_kernel(mine_ref, a_ref, b_ref, next_ref, prev_ref, own_ref):
    next_ref[...] = mine_ref[2] + a_ref[2]
    prev_ref[...] = mine_ref[0] + a_ref[0] + b_ref[1]
    own_ref[...] = mine_ref[1] + a_ref[1] + b_ref[0]


def add_far(mine, from_a, from_b):
    return pl.pallas_call(
        far_kernel,
        out_shape=(jax.ShapeDtypeStruct(mine.shape[1:], f32),) * 3,
        in_specs=[VMEM] * 3,
        out_specs=(VMEM,) * 3,
        compiler_params=pltpu.CompilerParams(vmem_limit_bytes=2 * MB),
        name="add_far",
    )(mine, from_a, from_b)


def reduce_rows(send, keep, after):
    own, *parts = add_core(keep, swap(send, "c"))
    moved = [shift(parts[d - 1], "y", d) for d in (1, 3, 2)]
    own, part = add_ring(own, moved, after)
    ahead, behind, mine = split_features(own, swap(part, "x"))
    from_a, from_b = shift(ahead, "z", 3), shift(behind, "z", 6)
    to_next, to_prev, own = add_far(mine, from_a, from_b)
    return own + shift(to_next, "z", 1) + shift(to_prev, "z", 7)


def per_device(hidden_student, hidden_teacher, targets, w_student, w_teacher):
    micro, tokens, _ = hidden_student.shape
    rows = micro * tokens
    block = join(hidden_student.reshape(rows, -1), hidden_teacher.reshape(rows, -1))
    tgt, pick = row_order(targets)
    early, (sides, far), tgt = gather_rows(block, tgt)
    s_early, t_early, h_early, part = compute_logits(early, w_student, w_teacher, tgt)
    sides, part = lax.optimization_barrier((sides, part))
    sides_swapped = swap(sides, "c")
    far, sides_swapped = lax.optimization_barrier((far, sides_swapped))
    late = sides, sides_swapped, far, swap(far, "c")
    s_late, t_late, h_late, part = compute_logits(late, w_student, w_teacher, tgt, (part, pick))
    parts = exchange_totals(part)
    s, t = (s_early, s_late), (t_early, t_late)
    g, send, keep, loss = compute_slope(s, t, parts, pick, tgt, w_student)
    grad_weight, done = compute_weight(g, h_early, h_late)
    grad_hidden = reduce_rows(send, keep, done)
    return loss, grad_hidden.astype(bf16).reshape(micro, tokens, -1), grad_weight


def solution(mesh):
    sec = ("y", "x", "c")
    devices = np.asarray(mesh.devices).reshape(RING_Y, PAIR_X, CORES, RING_Z, -1)
    fine = Mesh(devices, sec + ("z", "dp"))
    return jax.shard_map(
        per_device,
        mesh=fine,
        in_specs=(
            P("dp", sec, None),
            P("dp", sec, None),
            P("dp", None),
            P(sec + ("z",), None),
            P(sec + ("z",), None),
        ),
        out_specs=(P("dp"), P("dp", sec, "z"), P(("dp",) + sec + ("z",), None)),
        check_vma=False,
    )
```
